32 devices in a mesh: sub: 4 (over y, x), line: 8 (over z, core).
Axes of the slice: x: 2, y: 2, z: 4, core: 2. Of those that a mesh axis runs over, the one named last changes fastest.
Arguments:
- nodal_inverse: float32 [4, 128, 36864], P('sub', 'line'), may hold values from -1 to 1
- bus_source: float32 [4, 16, 12, 2048], P('sub', None, None, 'line'), may hold values from -16 to 16
- modal_map: float32 [12, 12], replicated, may hold values from -1.75 to 1.75
- admittance: float32 [4, 12, 2048], P('sub', None, 'line'), may hold values from 0.5 to 1.5
- attenuation: float32 [4, 12, 2048], P('sub', None, 'line'), may hold values from 0.6 to 0.95
- past_waves: float32 [4, 12, 12, 2048], P('sub', None, None, 'line'), may hold values from -6 to 6
- tie_code: int32 [8], P('line'), may hold values from 1 to 3, as said below
- travel_span: int32 [4, 2048], P('sub', 'line'), may hold values from 4 to 12, as said below
- bus_owner: int32 [4, 2048, 1], P('sub', 'line'), may hold values from 0 to 7; in each aligned block of 256 rows (0 to 255, 256 to 511, ..., all dimensions but the last counted through in order) at most 64 rows name the same one
- bus_local: int32 [4, 2048], P('sub', 'line'), may hold values from 0 to 255
- bus_count: int32 [4, 128], P('sub', 'line'), may hold values from 8 to 16
Outputs:
- volts: float32 [4, 16, 12, 2048], P('sub', None, None, 'line')
The draws below stay inside these ranges and needn't reach their ends.
Inputs may be any that keep to these rules, and one draw needn't show every extreme that they name: Index s of the sub axis and index s XOR tie_code[l] are partners in column l. A line has the same travel time at both of its ends: travel_span[s, j] equals travel_span[partner(s, j), j]. `bus_owner`: among the 256 line ends of one device, at most 64 name the same owner.
All inputs are finite; a program needn't handle non-finite values.
Results may differ from the reference program's by a relative error of at most 0.0001.
Values sent between devices are 32-bit elements; how exact they have to be, the bound alone decides.
A program may use at most 64 MiB of HBM per device.

```python
import math
import jax
import jax.numpy as jnp
import numpy as np
from jax import lax

COND = 12
NB = 16
LINE_DEV = 256
STEPS = 16
TMIN = 4
TMAX = 12
NODES = 192
BUS_DEV = 256
SUBS = 128
BUSES = 2048
LINES = 2048
CAP = 64
N_SUB = 4
N_LINE = 8


def common_codes(key):
    base_key = jax.random.fold_in(key, 11)
    codes = jax.random.randint(jax.random.fold_in(base_key, 1), (N_LINE,), 1, N_SUB)
    first_at = jax.random.randint(jax.random.fold_in(base_key, 2), (), 0, N_LINE)
    second_at = (first_at + 1 + jax.random.randint(jax.random.fold_in(base_key, 3), (), 0, N_LINE - 1)) % N_LINE
    return codes.at[first_at].set(1).at[second_at].set(N_SUB - 1)


def draw_tie_code(key, part):
    return common_codes(key).astype(jnp.int32)


def draw_travel_span(key, part):
    codes = common_codes(key)
    spans_base = jax.random.randint(jax.random.fold_in(key, 23), (N_SUB, LINES), TMIN, TMAX + 1)
    lowest_at = jax.random.randint(jax.random.fold_in(key, 29), (), 0, LINES)
    highest_at = (lowest_at + 1 + jax.random.randint(jax.random.fold_in(key, 31), (), 0, LINES - 1)) % LINES
    spans_base = spans_base.at[:, lowest_at].set(TMIN).at[:, highest_at].set(TMAX)
    rows_index = jnp.arange(N_SUB, dtype=jnp.int32)[:, None]
    column_code = codes[jnp.arange(LINES, dtype=jnp.int32) // LINE_DEV]
    pair_row = jnp.minimum(rows_index, jnp.bitwise_xor(rows_index, column_code[None, :]))
    return jnp.take_along_axis(spans_base, pair_row, axis=0).astype(jnp.int32)


def draw_bus_count(key, part):
    total = N_SUB * SUBS
    flat_counts = jax.random.randint(jax.random.fold_in(key, 41), (total,), NB // 2, NB + 1)
    highest_at = jax.random.randint(jax.random.fold_in(key, 43), (), 0, total)
    lowest_at = (highest_at + 1 + jax.random.randint(jax.random.fold_in(key, 47), (), 0, total - 1)) % total
    flat_counts = flat_counts.at[highest_at].set(NB).at[lowest_at].set(NB // 2)
    return flat_counts.reshape(N_SUB, SUBS).astype(jnp.int32)


def draw_nodal_inverse(key, part):
    shape_full = (N_SUB, SUBS, NODES, NODES)
    off_part = jax.random.normal(jax.random.fold_in(key, 53), shape_full, jnp.float32) * 0.003
    diag_part = jax.random.uniform(jax.random.fold_in(key, 59), (N_SUB, SUBS, NODES), jnp.float32, 0.06, 0.12)
    identity = jnp.eye(NODES, dtype=jnp.float32)
    square = off_part * (1.0 - identity) + diag_part[..., None] * identity
    return square.reshape(N_SUB, SUBS, NODES * NODES)


def plant(drawn, stream_key, smallest, top_value):
    shape = drawn.shape
    index_at = [jax.random.randint(jax.random.fold_in(stream_key, axis), (), 0, shape[axis]) for axis in range(len(shape))]
    drawn = drawn.at[tuple(index_at)].set(smallest)
    longest = shape.index(max(shape))
    index_at[longest] = (index_at[longest] + 1) % shape[longest]
    return drawn.at[tuple(index_at)].set(top_value)


def levels(key, dims, pieces, low, top_value):
    factor_of, own = 1.0, jax.random.fold_in(key, 6)
    for axis_at, shards_of in pieces:
        heights = jnp.exp(jax.random.uniform(jax.random.fold_in(own, axis_at), (shards_of,), jnp.float32, low / len(pieces), top_value / len(pieces)))
        factor_of = factor_of * jnp.repeat(heights, dims[axis_at] // shards_of).reshape([-1 if axis == axis_at else 1 for axis in range(len(dims))])
    return factor_of


def assign_block(key, own, number, rows, amount, top, most, slope):
    ranking = jax.random.permutation(key, amount)
    packed, common = load_shares(amount, rows * top, most, slope, True), load_shares(amount, rows * top, most, slope, False)
    places = jnp.arange(amount)

    def named(sizes, turn):
        used = int((sizes > 0).sum())
        fixed = max(1, used // 4)
        moved = fixed + (places - fixed + turn * (used - fixed)) % max(1, amount - fixed)
        return jnp.zeros((amount,), jnp.int32).at[ranking[jnp.where(places < fixed, places, moved)]].set(jnp.asarray(sizes, jnp.int32))

    sizes = jnp.where(number % 4 == 0, named(packed, number // 4), named(common, number - number // 4 - 1))
    mixed = jax.random.permutation(jax.random.fold_in(own, 3), amount)
    giver, receiver = mixed[0:amount // 2 * 2:2], mixed[1:amount // 2 * 2:2]
    room = jnp.minimum(sizes[giver] - 1, most - sizes[receiver]) // 2
    room = jnp.where((giver == ranking[0]) | (receiver == ranking[0]) | (sizes[receiver] == 0), 0, jnp.maximum(room, 0))
    moved = jax.random.randint(jax.random.fold_in(own, 4), (amount // 2,), 0, 1 << 20) % (room + 1)
    sizes = sizes.at[giver].add(-moved).at[receiver].add(moved)
    items = jnp.searchsorted(jnp.cumsum(sizes), jnp.arange(rows * top), side="right").astype(jnp.int32)
    table = items.reshape(top, rows).T
    table = table[jax.random.permutation(jax.random.fold_in(own, 1), rows)]
    turn = jax.random.randint(jax.random.fold_in(own, 2), (rows, 1), 0, top)
    return jnp.take_along_axis(table, (jnp.arange(top)[None, :] + turn) % top, axis=1)


def load_shares(count, total, reach, slope, full):
    loads = [(1 << 20) // math.isqrt(grade ** slope) + 1 for grade in range(1, count + 1)]
    largest = reach if full else min(reach, max(-(-total // count), total * loads[0] // sum(loads)))
    least = 1 if total - largest >= count - 1 else 0
    counts, spare = [largest] + [least] * (count - 1), total - largest - least * (count - 1)
    while spare > 0:
        free = [i for i in range(1, count) if counts[i] < largest] or [i for i in range(1, count) if counts[i] < reach]
        mass, remaining = sum([loads[i] for i in free]), spare
        for i in free:
            extra = min(reach - counts[i], max(1, remaining * loads[i] // mass), spare)
            counts[i] = counts[i] + extra
            spare = spare - extra
    return np.array(counts)


def scatter_about(stream_key, extent, scale, limit, cuts=(), kind=jnp.bfloat16):
    array = scale * jax.random.normal(stream_key, extent, jnp.float32)
    if cuts:
        array = array * levels(stream_key, extent, cuts, -0.22, 0.18)
    return jnp.clip(array, -limit, limit).astype(kind)


def setup_inputs(seed: int = 0) -> dict:
    key_list = jax.random.split(jax.random.key(seed), 12)
    nodal_inverse = draw_nodal_inverse(jax.random.fold_in(key_list[11], 71), 0)
    bus_source = scatter_about(key_list[1], (N_SUB, STEPS, COND, BUSES), 4.0, 16.0, ((0, 4), (3, 8)), jnp.float32)
    modal_map = scatter_about(key_list[2], (COND, COND), COND ** -0.5, 1.75, (), jnp.float32)
    admittance = jnp.clip(jnp.exp(math.log(1.5) - 1.0986123 * jax.random.uniform(key_list[3], (N_SUB, COND, LINES), jnp.float32) ** levels(key_list[3], (N_SUB, COND, LINES), ((0, 4), (2, 8)), -0.2, 0.2)), 0.5, 1.5)
    attenuation = jnp.clip(0.6 + 0.34999996 * jax.random.uniform(key_list[4], (N_SUB, COND, LINES), jnp.float32) ** levels(key_list[4], (N_SUB, COND, LINES), ((0, 4), (2, 8)), -0.2, 0.2), 0.6, 0.95)
    past_waves = scatter_about(key_list[5], (N_SUB, TMAX, COND, LINES), 1.0, 6.0, ((0, 4), (3, 8)), jnp.float32)
    tie_code = draw_tie_code(jax.random.fold_in(key_list[11], 71), 0)
    travel_span = draw_travel_span(jax.random.fold_in(key_list[11], 71), 0)
    bus_owner_keys = jax.random.split(jax.random.fold_in(key_list[8], 1), N_SUB * LINES // LINE_DEV)
    bus_owner_turns = jax.random.permutation(jax.random.fold_in(key_list[8], 3), N_SUB * LINES // LINE_DEV)
    bus_owner = jax.vmap(lambda own, number: assign_block(jax.random.fold_in(key_list[8], 2), own, number, LINE_DEV, N_LINE, 1, CAP, 2))(bus_owner_keys, bus_owner_turns).reshape((N_SUB, LINES, 1))
    bus_local = plant(jax.random.randint(key_list[9], (N_SUB, LINES), 0, BUS_DEV), jax.random.fold_in(key_list[9], 1), 0, BUS_DEV - 1).astype(jnp.int32)
    bus_count = draw_bus_count(jax.random.fold_in(key_list[11], 71), 0)
    return dict(nodal_inverse=nodal_inverse, bus_source=bus_source, modal_map=modal_map, admittance=admittance, attenuation=attenuation, past_waves=past_waves, tie_code=tie_code, travel_span=travel_span, bus_owner=bus_owner, bus_local=bus_local, bus_count=bus_count)


def reference(nodal_inverse, bus_source, modal_map, admittance, attenuation, past_waves, tie_code, travel_span, bus_owner, bus_local, bus_count):
    highest = lax.Precision.HIGHEST
    nodal_square = nodal_inverse.reshape(N_SUB, SUBS, NODES, NODES)
    line_col = jnp.arange(LINES, dtype=jnp.int32) // LINE_DEV
    groups = jnp.arange(N_SUB, dtype=jnp.int32)
    partner = jnp.bitwise_xor(groups[:, None], tie_code[line_col][None, :]).astype(jnp.int32)
    partner_full = jnp.broadcast_to(partner[:, None, :], (N_SUB, COND, LINES))
    bus_index = (bus_owner[:, :, 0] * BUS_DEV + bus_local).astype(jnp.int32)
    bus_full = jnp.broadcast_to(bus_index[:, None, :], (N_SUB, COND, LINES))
    flat_index = (groups[:, None] * BUSES + bus_index).reshape(-1)
    live_bus = (jnp.arange(NB, dtype=jnp.int32)[None, None, :] < bus_count[:, :, None]).astype(jnp.float32).reshape(N_SUB, 1, BUSES)
    timeline = jnp.concatenate([past_waves, jnp.zeros((N_SUB, STEPS, COND, LINES), jnp.float32)], axis=1)
    volt_list = []
    for instant in range(STEPS):
        where_from = (instant + TMAX - travel_span).astype(jnp.int32)
        where_full = jnp.broadcast_to(where_from[:, None, None, :], (N_SUB, 1, COND, LINES))
        arrived = jnp.take_along_axis(timeline, where_full, axis=1)[:, 0]
        history = attenuation * arrived
        inject = jnp.einsum("cm,sml->scl", modal_map, history, precision=highest)
        summed = jax.ops.segment_sum(jnp.transpose(inject, (0, 2, 1)).reshape(N_SUB * LINES, COND), flat_index, num_segments=N_SUB * BUSES)
        right_side = (bus_source[:, instant] + jnp.transpose(summed.reshape(N_SUB, BUSES, COND), (0, 2, 1))) * live_bus
        stacked = jnp.transpose(right_side.reshape(N_SUB, COND, SUBS, NB), (0, 2, 1, 3)).reshape(N_SUB, SUBS, NODES)
        solved = jnp.einsum("sgij,sgj->sgi", nodal_square, stacked, precision=highest)
        voltage = jnp.transpose(solved.reshape(N_SUB, SUBS, COND, NB), (0, 2, 1, 3)).reshape(N_SUB, COND, BUSES) * live_bus
        volt_list.append(voltage)
        at_lines = jnp.take_along_axis(voltage, bus_full, axis=2)
        modal_volts = jnp.einsum("cm,scl->sml", modal_map, at_lines, precision=highest)
        outgoing = 2.0 * admittance * modal_volts - history
        timeline = timeline.at[:, TMAX + instant].set(jnp.take_along_axis(outgoing, partner_full, axis=0))
    return jnp.stack(volt_list, axis=1)
```

```python
import functools

import jax
import jax.numpy as jnp
from jax import lax
from jax.experimental import pallas as pl
from jax.experimental.pallas import tpu as pltpu
from jax.sharding import PartitionSpec as P

TMIN = 4
PAD = 16
ROWS = TMIN * PAD
BF = jnp.bfloat16
F32 = jnp.float32
MESH = pl.DeviceIdType.MESH


def split(x):
    high = x.astype(BF)
    return high, (x - high.astype(F32)).astype(BF)


def mm(a, b):
    return jnp.dot(a, b, preferred_element_type=F32)


def pick(x, hot):
    high, low = split(x)
    both = mm(jnp.concatenate([high, low], axis=0), hot)
    return both[: x.shape[0]] + both[x.shape[0] :]


def apply_map(cat, x):
    high, low = split(x)
    return mm(cat, jnp.concatenate([high, high, low], axis=0))


def iota(shape, axis):
    return lax.broadcasted_iota(jnp.int32, shape, axis)


def kernel(
    n_line, n_sub, w_hbm, src, mmap, adm, att, past, code, span, owner, local, counts, out,
    w_flat, w_split, timeline, p_hot, pt_hot, q_hot, qt_hot, spread, map_cat, mapt_cat,
    source, admit, hist, inj_send, inj_recv, v_send, v_recv, sub_send, sub_recv,
    w_sem, inj_ss, inj_rs, v_ss, v_rs, sub_ss, sub_rs,
):
    me = lax.axis_index("line")
    grp = lax.axis_index("sub")
    steps, cond, buses = src.shape[1:]
    lines = adm.shape[2]
    depth = past.shape[1]
    subsets = w_hbm.shape[1]
    per = buses // subsets
    nodes = cond * per
    blocks = steps // TMIN
    cap = 2 * lines // n_line
    slots = n_line * cap
    parts = 128 // cap
    prow = ROWS // parts

    barrier = pltpu.get_barrier_semaphore()
    for k in range(1, n_line):
        pl.semaphore_signal(
            barrier, inc=1, device_id={"line": lax.rem(me + k, n_line)}, device_id_type=MESH
        )
    for k in range(1, n_sub):
        pl.semaphore_signal(
            barrier, inc=1, device_id={"sub": lax.rem(grp + k, n_sub)}, device_id_type=MESH
        )
    w_copy = pltpu.make_async_copy(w_hbm.at[0], w_flat, w_sem)
    w_copy.start()

    def line_copy(send, recv, ss, rs, k):
        to = lax.rem(me + k, n_line)
        return pltpu.make_async_remote_copy(
            src_ref=send.at[to], dst_ref=recv.at[me], send_sem=ss.at[k], recv_sem=rs.at[k],
            device_id={"line": to}, device_id_type=MESH,
        )

    def line_wait(send, recv, ss, rs):
        for k in range(1, n_line):
            frm = lax.rem(me + n_line - k, n_line)
            pltpu.make_async_remote_copy(
                src_ref=send.at[frm], dst_ref=recv.at[frm], send_sem=ss.at[k], recv_sem=rs.at[k],
                device_id={"line": frm}, device_id_type=MESH,
            ).wait_recv()
        for k in range(1, n_line):
            line_copy(send, recv, ss, rs, k).wait_send()

    def pack(x, send, recv):
        for d in range(n_line):
            send[d] = jnp.concatenate(
                [x[g * prow : (g + 1) * prow, d * cap : (d + 1) * cap] for g in range(parts)], axis=1
            )
        recv[me] = send[me]

    def unpack(recv):
        return jnp.concatenate(
            [
                jnp.concatenate(
                    [recv[d][:, g * cap : (g + 1) * cap] for d in range(n_line)], axis=1
                )
                for g in range(parts)
            ],
            axis=0,
        )

    def sub_copy(parity, k):
        return pltpu.make_async_remote_copy(
            src_ref=sub_send, dst_ref=sub_recv.at[parity, k - 1],
            send_sem=sub_ss.at[parity, k - 1], recv_sem=sub_rs.at[parity, k - 1],
            device_id={"sub": lax.rem(grp + k, n_sub)}, device_id_type=MESH,
        )

    hot_t = (iota((PAD, lines), 0) == owner[...]).astype(F32)
    upper = (iota((lines, lines), 0) < iota((lines, lines), 1)).astype(F32).astype(BF)
    earlier = mm(hot_t.astype(BF), upper)
    base = (iota((PAD, lines), 0) * cap).astype(F32)
    slot_row = jnp.sum(hot_t * (base + earlier), axis=0, keepdims=True).astype(jnp.int32)
    pt = (iota((slots, lines), 0) == slot_row).astype(F32)
    pt_hot[...] = pt.astype(BF)
    p_hot[...] = pt.T.astype(BF)

    stretch = ((iota((ROWS, cond), 0) & (PAD - 1)) == iota((ROWS, cond), 1)).astype(F32)
    same = (iota((ROWS, ROWS), 0) // PAD == iota((ROWS, ROWS), 1) // PAD).astype(F32)
    highest = lax.Precision.HIGHEST
    nt = (((1,), (1,)), ((), ()))

    def full(x):
        return lax.dot_general(x, stretch, nt, precision=highest, preferred_element_type=F32) * same

    fwd = full(jnp.dot(stretch, mmap[...], precision=highest, preferred_element_type=F32))
    bwd = full(lax.dot_general(stretch, mmap[...], nt, precision=highest, preferred_element_type=F32))
    for ref, big in ((map_cat, fwd), (mapt_cat, bwd)):
        high, low = split(big)
        ref[...] = jnp.concatenate(
            [high.astype(F32), low.astype(F32), high.astype(F32)], axis=1
        ).astype(BF)

    timeline[...] = jnp.zeros_like(timeline)
    for i in range(depth):
        timeline[i * PAD : i * PAD + cond, :] = past[0, i]
    damp = jnp.concatenate([att[0], jnp.zeros((PAD - cond, lines), F32)], axis=0)
    span_row = span[...]

    def history(block):
        for t in range(TMIN):
            total = jnp.zeros((PAD, lines), F32)
            for d in range(depth - TMIN + 1):
                at = pl.multiple_of((block * TMIN + t + d) * PAD, PAD)
                total = jnp.where(span_row == depth - d, timeline[pl.ds(at, PAD), :], total)
            hist[t * PAD : (t + 1) * PAD, :] = damp * total

    def start_inject(extra):
        inject = apply_map(map_cat[...], hist[...])
        if extra is not None:
            inject = jnp.where(iota((ROWS, lines), 0) == cond, extra, inject)
        pack(pick(inject, p_hot[...]), inj_send, inj_recv)

    history(0)
    start_inject(local[...].astype(F32))
    pl.semaphore_wait(barrier, n_line - 1 + n_sub - 1)
    for k in range(1, n_line):
        line_copy(inj_send, inj_recv, inj_ss, inj_rs, k).start()

    r, s = iota((2 * ROWS, cond * 128), 0), iota((2 * ROWS, cond * 128), 1)
    spread[...] = (
        ((r // PAD) == ((s & 127) // PAD)) & ((r & (PAD - 1)) == s // 128)
    ).astype(F32).astype(BF)
    expand = (iota((subsets, buses), 0) == iota((subsets, buses), 1) // per).astype(F32).astype(BF)
    count_row = mm(
        jnp.broadcast_to(counts[...].astype(F32), (8, subsets)).astype(BF), expand
    )[0:1]
    slot_in = (iota((1, buses), 1) & (per - 1)).astype(F32)
    live = (slot_in < count_row).astype(F32)
    source[...] = jnp.zeros_like(source)
    for t in range(steps):
        source[t * PAD : t * PAD + cond, :] = src[0, t]
    admit[...] = jnp.concatenate(
        [2.0 * adm[0], jnp.zeros((PAD - cond, lines), F32)] * TMIN, axis=0
    )
    w_copy.wait()

    def relayout(n, carry):
        at = pl.multiple_of(n * (16 * nodes), 128)
        wide = w_flat[:, pl.ds(at, 16 * nodes)]
        cube = jnp.stack([wide[:, i * nodes : (i + 1) * nodes] for i in range(16)], axis=0)
        turned = jnp.transpose(cube, (1, 0, 2))
        high, low = split(turned)
        here = pl.multiple_of(n * 16, 16)
        w_split[:, pl.ds(here, 16), :] = high
        w_split[:, pl.ds(pl.multiple_of(nodes + here, 16), 16), :] = low
        return carry

    lax.fori_loop(0, nodes // 16, relayout, 0)
    partner = lax.bitwise_xor(grp, code[0])

    line_wait(inj_send, inj_recv, inj_ss, inj_rs)
    id_row = unpack(inj_recv)[cond : cond + 1, :]
    qt = (iota((buses, slots), 0).astype(F32) == id_row).astype(F32)
    qt_hot[...] = qt.astype(BF)
    q_hot[...] = qt.T.astype(BF)
    diag = iota((per, 128), 1) & (PAD - 1)

    def one_block(block, carry):
        at = pl.multiple_of(block * ROWS, ROWS)
        summed = pick(unpack(inj_recv), q_hot[...])
        right = (summed + source[pl.ds(at, ROWS), :]) * live
        high, low = split(right)
        both = jnp.concatenate([high.astype(F32), low.astype(F32)], axis=0)
        wide = mm(both.T.astype(BF), spread[...]).astype(BF)
        pieces = []
        for g in range(subsets):
            x = jnp.concatenate(
                [wide[g * per : (g + 1) * per, c * 128 : (c + 1) * 128] for c in range(cond)], axis=0
            )
            y = mm(w_split[g], x)
            y = y[:nodes] + y[nodes:]
            total = jnp.zeros((per, 128), F32)
            for c in range(cond):
                total = jnp.where(diag == c, y[c * per : (c + 1) * per], total)
            pieces.append(total)
        turned = jnp.concatenate(pieces, axis=0).T
        volts = (turned[:ROWS] + turned[ROWS:]) * live
        for t in range(TMIN):
            out[0, block * TMIN + t] = volts[t * PAD : t * PAD + cond]

        @pl.when(block < blocks - 1)
        def _():
            pack(pick(volts, qt_hot[...]), v_send, v_recv)
            for k in range(1, n_line):
                line_copy(v_send, v_recv, v_ss, v_rs, k).start()
            line_wait(v_send, v_recv, v_ss, v_rs)
            modal = apply_map(mapt_cat[...], pick(unpack(v_recv), pt_hot[...]))
            sub_send[...] = admit[...] * modal - hist[...]
            parity = lax.rem(block, 2)
            for k in range(1, n_sub):
                sub_copy(parity, k).start()
            arrived = jnp.zeros((ROWS, lines), F32)
            for k in range(1, n_sub):
                sub_copy(parity, k).wait_recv()
                frm = lax.rem(grp + n_sub - k, n_sub)
                arrived = jnp.where(partner == frm, sub_recv[parity, k - 1], arrived)
            for k in range(1, n_sub):
                sub_copy(parity, k).wait_send()
            timeline[pl.ds(pl.multiple_of((depth + block * TMIN) * PAD, PAD), ROWS), :] = arrived
            history(block + 1)
            start_inject(None)
            for k in range(1, n_line):
                line_copy(inj_send, inj_recv, inj_ss, inj_rs, k).start()
            line_wait(inj_send, inj_recv, inj_ss, inj_rs)

        return carry

    lax.fori_loop(0, blocks, one_block, 0)


def per_device(
    nodal_inverse, bus_source, modal_map, admittance, attenuation, past_waves, tie_code,
    travel_span, bus_owner, bus_local, bus_count,
):
    n_line, n_sub = lax.axis_size("line"), lax.axis_size("sub")
    _, steps, cond, buses = bus_source.shape
    lines = admittance.shape[2]
    depth = past_waves.shape[1]
    subsets = nodal_inverse.shape[1]
    nodes = cond * (buses // subsets)
    cap = 2 * lines // n_line
    slots = n_line * cap
    prow = ROWS * cap // 128
    vmem = pl.BlockSpec(memory_space=pltpu.VMEM)
    smem = pl.BlockSpec(memory_space=pltpu.SMEM)
    dma = pltpu.SemaphoreType.DMA
    return pl.pallas_call(
        functools.partial(kernel, n_line, n_sub),
        out_shape=jax.ShapeDtypeStruct(bus_source.shape, F32),
        in_specs=[pl.BlockSpec(memory_space=pl.ANY), vmem, vmem, vmem, vmem, vmem, smem, vmem,
                  vmem, vmem, vmem],
        out_specs=vmem,
        scratch_shapes=[
            pltpu.VMEM((subsets, nodes * nodes), F32),
            pltpu.VMEM((subsets, 2 * nodes, nodes), BF),
            pltpu.VMEM(((depth + steps) * PAD, lines), F32),
            pltpu.VMEM((lines, slots), BF),
            pltpu.VMEM((slots, lines), BF),
            pltpu.VMEM((slots, buses), BF),
            pltpu.VMEM((buses, slots), BF),
            pltpu.VMEM((2 * ROWS, cond * 128), BF),
            pltpu.VMEM((ROWS, 3 * ROWS), BF),
            pltpu.VMEM((ROWS, 3 * ROWS), BF),
            pltpu.VMEM((steps * PAD, buses), F32),
            pltpu.VMEM((ROWS, lines), F32),
            pltpu.VMEM((ROWS, lines), F32),
            pltpu.VMEM((n_line, prow, 128), F32),
            pltpu.VMEM((n_line, prow, 128), F32),
            pltpu.VMEM((n_line, prow, 128), F32),
            pltpu.VMEM((n_line, prow, 128), F32),
            pltpu.VMEM((ROWS, lines), F32),
            pltpu.VMEM((2, n_sub - 1, ROWS, lines), F32),
            dma,
            dma((n_line,)), dma((n_line,)), dma((n_line,)), dma((n_line,)),
            dma((2, n_sub - 1)), dma((2, n_sub - 1)),
        ],
        compiler_params=pltpu.CompilerParams(
            collective_id=0, has_side_effects=True, vmem_limit_bytes=40 * 1024 * 1024
        ),
    )(
        nodal_inverse, bus_source, modal_map, admittance, attenuation, past_waves, tie_code,
        travel_span, bus_owner[:, :, 0], bus_local, bus_count,
    )


def solution(mesh):
    in_specs = (
        P("sub", "line", None),
        P("sub", None, None, "line"),
        P(),
        P("sub", None, "line"),
        P("sub", None, "line"),
        P("sub", None, None, "line"),
        P("line"),
        P("sub", "line"),
        P("sub", "line", None),
        P("sub", "line"),
        P("sub", "line"),
    )
    out_specs = P("sub", None, None, "line")
    return jax.shard_map(
        per_device, mesh=mesh, in_specs=in_specs, out_specs=out_specs, check_vma=False
    )
```

```python
import functools

import jax
import jax.numpy as jnp
from jax import lax
from jax.experimental import pallas as pl
from jax.experimental.pallas import tpu as pltpu
from jax.sharding import PartitionSpec as P

TMIN = 4
PAD = 16
WIDE = 64
BF = jnp.bfloat16
F32 = jnp.float32
MESH = pl.DeviceIdType.MESH


def split(x):
    high = x.astype(BF)
    return high, (x - high.astype(F32)).astype(BF)


def mm(a, b):
    return jnp.dot(a, b, preferred_element_type=F32)


def pick(x, hot):
    high, low = split(x)
    both = mm(jnp.concatenate([high, low], axis=0), hot)
    return both[: x.shape[0]] + both[x.shape[0] :]


def apply_map(cat, x):
    high, low = split(x)
    return mm(cat, jnp.concatenate([high, high, low], axis=0))


def iota(shape, axis):
    return lax.broadcasted_iota(jnp.int32, shape, axis)


def kernel(
    n_line, n_sub, w_hbm, src_in, mmap_in, adm_in, att_in, past_in, code, span_in, owner_in,
    local_in, counts_in, out,
    src, mmap, adm, att, past, span, owner, local, counts, in_sem,
    w_flat, w_split, timeline, p_hot, pt_hot, q_hot, qt_hot, spread, map_cat, mapt_cat,
    source, admit, hist, inj_send, inj_recv, v_send, v_recv, sub_send, sub_recv,
    w_sem, inj_ss, inj_rs, v_ss, v_rs, sub_ss, sub_rs,
):
    me = lax.axis_index("line")
    grp = lax.axis_index("sub")
    cond, steps, buses = src.shape[1:]
    rows = TMIN * cond
    lines = adm.shape[2]
    depth = past.shape[1]
    subsets = w_hbm.shape[1]
    per = buses // subsets
    nodes = cond * per
    blocks = steps // TMIN
    cap = 2 * lines // n_line
    slots = n_line * cap
    parts = 128 // cap
    prow = rows // parts
    sent = -(-prow // 8) * 8

    barrier = pltpu.get_barrier_semaphore()
    for k in range(1, n_line):
        pl.semaphore_signal(
            barrier, inc=1, device_id={"line": lax.rem(me + k, n_line)}, device_id_type=MESH
        )
    for k in range(1, n_sub):
        pl.semaphore_signal(
            barrier, inc=1, device_id={"sub": lax.rem(grp + k, n_sub)}, device_id_type=MESH
        )
    w_copy = pltpu.make_async_copy(w_hbm.at[0], w_flat, w_sem)
    loads = [
        pltpu.make_async_copy(a, b, in_sem.at[i])
        for i, (a, b) in enumerate(
            [(owner_in, owner), (local_in, local), (span_in, span), (mmap_in, mmap), (past_in, past),
             (att_in, att), (adm_in, adm), (src_in, src), (counts_in, counts)]
        )
    ]
    for load in loads:
        load.start()
    w_copy.start()
    for load in loads[:6]:
        load.wait()

    def line_copy(send, recv, ss, rs, k, high=None):
        high = sent if high is None else high
        to = lax.rem(me + k, n_line)
        return pltpu.make_async_remote_copy(
            src_ref=send.at[to, 0:high], dst_ref=recv.at[me, 0:high], send_sem=ss.at[k], recv_sem=rs.at[k],
            device_id={"line": to}, device_id_type=MESH,
        )

    def line_wait(send, recv, ss, rs, high=None):
        high = sent if high is None else high
        for k in range(1, n_line):
            frm = lax.rem(me + n_line - k, n_line)
            pltpu.make_async_remote_copy(
                src_ref=send.at[frm, 0:high], dst_ref=recv.at[frm, 0:high], send_sem=ss.at[k], recv_sem=rs.at[k],
                device_id={"line": frm}, device_id_type=MESH,
            ).wait_recv()

    def line_sent(send, recv, ss, rs, high=None):
        for k in range(1, n_line):
            line_copy(send, recv, ss, rs, k, high).wait_send()

    def pack(x, send, recv):
        for d in range(n_line):
            send[d, 0:prow] = jnp.concatenate(
                [x[g * prow : (g + 1) * prow, d * cap : (d + 1) * cap] for g in range(parts)], axis=1
            )
        recv[me, 0:prow] = send[me, 0:prow]

    def unpack(recv):
        return jnp.concatenate(
            [
                jnp.concatenate(
                    [recv[d, 0:prow][:, g * cap : (g + 1) * cap] for d in range(n_line)], axis=1
                )
                for g in range(parts)
            ],
            axis=0,
        )

    def sub_copy(parity, k):
        return pltpu.make_async_remote_copy(
            src_ref=sub_send, dst_ref=sub_recv.at[parity, k - 1],
            send_sem=sub_ss.at[parity, k - 1], recv_sem=sub_rs.at[parity, k - 1],
            device_id={"sub": lax.rem(grp + k, n_sub)}, device_id_type=MESH,
        )

    hot_t = (iota((PAD, lines), 0) == owner[...]).astype(F32)
    upper = (iota((lines, lines), 0) < iota((lines, lines), 1)).astype(F32).astype(BF)
    earlier = mm(hot_t.astype(BF), upper)
    base = (iota((PAD, lines), 0) * cap).astype(F32)
    slot_row = jnp.sum(hot_t * (base + earlier), axis=0, keepdims=True).astype(jnp.int32)
    pt = (iota((slots, lines), 0) == slot_row).astype(F32)
    pt_hot[...] = pt.astype(BF)
    p_hot[...] = pt.T.astype(BF)

    stretch = (iota((rows, cond), 0) % cond == iota((rows, cond), 1)).astype(F32)
    same = (iota((rows, rows), 0) // cond == iota((rows, rows), 1) // cond).astype(F32)
    highest = lax.Precision.HIGHEST
    nt = (((1,), (1,)), ((), ()))

    def full(x):
        return lax.dot_general(x, stretch, nt, precision=highest, preferred_element_type=F32) * same

    fwd = full(jnp.dot(stretch, mmap[...], precision=highest, preferred_element_type=F32))
    bwd = full(lax.dot_general(stretch, mmap[...], nt, precision=highest, preferred_element_type=F32))
    for ref, big in ((map_cat, fwd), (mapt_cat, bwd)):
        high, low = split(big)
        ref[...] = jnp.concatenate(
            [high.astype(F32), low.astype(F32), high.astype(F32)], axis=1
        ).astype(BF)

    timeline[...] = jnp.zeros_like(timeline)
    for i in range(depth):
        timeline[i * PAD : i * PAD + cond, :] = past[0, i]
    damp = jnp.concatenate([att[0], jnp.zeros((PAD - cond, lines), F32)], axis=0)
    span_row = span[...]

    def history(block):
        for t in range(TMIN):
            total = jnp.zeros((PAD, lines), F32)
            for d in range(depth - TMIN + 1):
                at = pl.multiple_of((block * TMIN + t + d) * PAD, PAD)
                total = jnp.where(span_row == depth - d, timeline[pl.ds(at, PAD), :], total)
            hist[t * cond : (t + 1) * cond, :] = (damp * total)[:cond]

    def start_inject(extra):
        inject = apply_map(map_cat[...], hist[...])
        if extra is not None:
            both = jnp.concatenate([inject, jnp.broadcast_to(extra, (16, lines))], axis=0)
            both = pick(both, p_hot[...])
            inject = both[:rows]
            for d in range(n_line):
                piece = both[rows : rows + 8, d * cap : (d + 1) * cap]
                inj_send[d, sent : sent + 8] = jnp.concatenate([piece] * parts, axis=1)
            inj_recv[me, sent : sent + 8] = inj_send[me, sent : sent + 8]
        else:
            inject = pick(inject, p_hot[...])
        pack(inject, inj_send, inj_recv)

    history(0)
    if sent > prow:
        inj_send[...] = jnp.zeros_like(inj_send)
        v_send[...] = jnp.zeros_like(v_send)
    start_inject(local[...].astype(F32))
    pl.semaphore_wait(barrier, n_line - 1 + n_sub - 1)
    for k in range(1, n_line):
        line_copy(inj_send, inj_recv, inj_ss, inj_rs, k, sent + 8).start()

    for load in loads[6:]:
        load.wait()
    r, s = iota((2 * WIDE, cond * 128), 0), iota((2 * WIDE, cond * 128), 1)
    r_in, s_in = r & (WIDE - 1), s & (WIDE - 1)
    spread[...] = (
        (r // WIDE == (s & 127) // WIDE) & (r_in // cond == s_in // cond)
        & (r_in % cond == s // 128)
    ).astype(F32).astype(BF)
    expand = (iota((subsets, buses), 0) == iota((subsets, buses), 1) // per).astype(F32).astype(BF)
    count_row = mm(
        jnp.broadcast_to(counts[...].astype(F32), (8, subsets)).astype(BF), expand
    )[0:1]
    slot_in = (iota((1, buses), 1) & (per - 1)).astype(F32)
    live = (slot_in < count_row).astype(F32)
    for t in range(steps):
        source[t * cond : (t + 1) * cond, :] = src[0, :, t, :]
    admit[...] = jnp.concatenate([2.0 * adm[0]] * TMIN, axis=0)
    w_copy.wait()

    def relayout(n, carry):
        at = pl.multiple_of(n * (16 * nodes), 128)
        wide = w_flat[:, pl.ds(at, 16 * nodes)]
        cube = jnp.stack([wide[:, i * nodes : (i + 1) * nodes] for i in range(16)], axis=0)
        turned = jnp.transpose(cube, (1, 0, 2))
        high, low = split(turned)
        here = pl.multiple_of(n * 16, 16)
        w_split[:, pl.ds(here, 16), :] = high
        w_split[:, pl.ds(pl.multiple_of(nodes + here, 16), 16), :] = low
        return carry

    lax.fori_loop(0, nodes // 16, relayout, 0)
    partner = lax.bitwise_xor(grp, code[0])

    line_wait(inj_send, inj_recv, inj_ss, inj_rs, sent + 8)
    line_sent(inj_send, inj_recv, inj_ss, inj_rs, sent + 8)
    id_row = jnp.concatenate(
        [inj_recv[d, sent : sent + 8][0:1, 0:cap] for d in range(n_line)], axis=1
    )
    qt = (iota((buses, slots), 0).astype(F32) == id_row).astype(F32)
    qt_hot[...] = qt.astype(BF)
    q_hot[...] = qt.T.astype(BF)
    diag = (iota((per, 128), 1) & (WIDE - 1)) % cond

    def one_block(block, carry):
        at = pl.multiple_of(block * rows, 8)
        summed = pick(unpack(inj_recv), q_hot[...])
        right = (summed + source[pl.ds(at, rows), :]) * live
        high, low = split(right)
        gap = jnp.zeros((WIDE - rows, buses), F32)
        both = jnp.concatenate([high.astype(F32), gap, low.astype(F32), gap], axis=0)
        wide = mm(both.T.astype(BF), spread[...]).astype(BF)
        pieces = []
        for g in range(subsets):
            x = jnp.concatenate(
                [wide[g * per : (g + 1) * per, c * 128 : (c + 1) * 128] for c in range(cond)], axis=0
            )
            y = mm(w_split[g], x)
            y = y[:nodes] + y[nodes:]
            total = jnp.zeros((per, 128), F32)
            for c in range(cond):
                total = jnp.where(diag == c, y[c * per : (c + 1) * per], total)
            pieces.append(total)
        turned = jnp.concatenate(pieces, axis=0).T
        volts = (turned[:rows] + turned[WIDE : WIDE + rows]) * live
        for t in range(TMIN):
            out[0, block * TMIN + t] = volts[t * cond : (t + 1) * cond]

        @pl.when(block < blocks - 1)
        def _():
            pack(pick(volts, qt_hot[...]), v_send, v_recv)
            for k in range(1, n_line):
                line_copy(v_send, v_recv, v_ss, v_rs, k).start()
            line_wait(v_send, v_recv, v_ss, v_rs)
            modal = apply_map(mapt_cat[...], pick(unpack(v_recv), pt_hot[...]))
            sub_send[...] = admit[...] * modal - hist[...]
            parity = lax.rem(block, 2)
            for k in range(1, n_sub):
                sub_copy(parity, k).start()
            arrived = jnp.zeros((rows, lines), F32)
            for k in range(1, n_sub):
                sub_copy(parity, k).wait_recv()
                frm = lax.rem(grp + n_sub - k, n_sub)
                arrived = jnp.where(partner == frm, sub_recv[parity, k - 1], arrived)
            gap = jnp.zeros((PAD - cond, lines), F32)
            for t in range(TMIN):
                here = pl.multiple_of((depth + block * TMIN + t) * PAD, PAD)
                timeline[pl.ds(here, PAD), :] = jnp.concatenate(
                    [arrived[t * cond : (t + 1) * cond], gap], axis=0
                )
            history(block + 1)
            start_inject(None)
            for k in range(1, n_line):
                line_copy(inj_send, inj_recv, inj_ss, inj_rs, k).start()
            line_sent(v_send, v_recv, v_ss, v_rs)
            for k in range(1, n_sub):
                sub_copy(parity, k).wait_send()
            line_wait(inj_send, inj_recv, inj_ss, inj_rs)
            line_sent(inj_send, inj_recv, inj_ss, inj_rs)

        return carry

    lax.fori_loop(0, blocks, one_block, 0)


def per_device(
    nodal_inverse, bus_source, modal_map, admittance, attenuation, past_waves, tie_code,
    travel_span, bus_owner, bus_local, bus_count,
):
    n_line, n_sub = lax.axis_size("line"), lax.axis_size("sub")
    _, steps, cond, buses = bus_source.shape
    lines = admittance.shape[2]
    depth = past_waves.shape[1]
    subsets = nodal_inverse.shape[1]
    nodes = cond * (buses // subsets)
    cap = 2 * lines // n_line
    slots = n_line * cap
    rows = TMIN * cond
    sent = -(-(rows * cap // 128) // 8) * 8
    vmem = pl.BlockSpec(memory_space=pltpu.VMEM)
    hbm = pl.BlockSpec(memory_space=pl.ANY)
    smem = pl.BlockSpec(memory_space=pltpu.SMEM)
    dma = pltpu.SemaphoreType.DMA
    return pl.pallas_call(
        functools.partial(kernel, n_line, n_sub),
        out_shape=jax.ShapeDtypeStruct(bus_source.shape, F32),
        in_specs=[hbm] * 6 + [smem] + [hbm] * 4,
        out_specs=vmem,
        scratch_shapes=[
            pltpu.VMEM((1, cond, steps, buses), F32),
            pltpu.VMEM((cond, cond), F32),
            pltpu.VMEM((1, cond, lines), F32),
            pltpu.VMEM((1, cond, lines), F32),
            pltpu.VMEM((1, depth, cond, lines), F32),
            pltpu.VMEM((1, lines), jnp.int32),
            pltpu.VMEM((1, lines), jnp.int32),
            pltpu.VMEM((1, lines), jnp.int32),
            pltpu.VMEM((1, subsets), jnp.int32),
            dma((9,)),
            pltpu.VMEM((subsets, nodes * nodes), F32),
            pltpu.VMEM((subsets, 2 * nodes, nodes), BF),
            pltpu.VMEM(((depth + steps) * PAD, lines), F32),
            pltpu.VMEM((lines, slots), BF),
            pltpu.VMEM((slots, lines), BF),
            pltpu.VMEM((slots, buses), BF),
            pltpu.VMEM((buses, slots), BF),
            pltpu.VMEM((2 * WIDE, cond * 128), BF),
            pltpu.VMEM((rows, 3 * rows), BF),
            pltpu.VMEM((rows, 3 * rows), BF),
            pltpu.VMEM((steps * cond, buses), F32),
            pltpu.VMEM((rows, lines), F32),
            pltpu.VMEM((rows, lines), F32),
            pltpu.VMEM((n_line, sent + 8, 128), F32),
            pltpu.VMEM((n_line, sent + 8, 128), F32),
            pltpu.VMEM((n_line, sent, 128), F32),
            pltpu.VMEM((n_line, sent, 128), F32),
            pltpu.VMEM((rows, lines), F32),
            pltpu.VMEM((2, n_sub - 1, rows, lines), F32),
            dma,
            dma((n_line,)), dma((n_line,)), dma((n_line,)), dma((n_line,)),
            dma((2, n_sub - 1)), dma((2, n_sub - 1)),
        ],
        compiler_params=pltpu.CompilerParams(
            collective_id=0, has_side_effects=True, vmem_limit_bytes=56 * 1024 * 1024
        ),
    )(
        nodal_inverse, jnp.transpose(bus_source, (0, 2, 1, 3)), modal_map, admittance, attenuation,
        past_waves, tie_code, travel_span, bus_owner[:, :, 0], bus_local, bus_count,
    )


def solution(mesh):
    in_specs = (
        P("sub", "line", None),
        P("sub", None, None, "line"),
        P(),
        P("sub", None, "line"),
        P("sub", None, "line"),
        P("sub", None, None, "line"),
        P("line"),
        P("sub", "line"),
        P("sub", "line", None),
        P("sub", "line"),
        P("sub", "line"),
    )
    out_specs = P("sub", None, None, "line")
    return jax.shard_map(
        per_device, mesh=mesh, in_specs=in_specs, out_specs=out_specs, check_vma=False
    )
```

```python
import functools

import jax
import jax.numpy as jnp
from jax import lax
from jax.experimental import pallas as pl
from jax.experimental.pallas import tpu as pltpu
from jax.sharding import PartitionSpec as P

TMIN = 4
PAD = 16
WIDE = 64
BF = jnp.bfloat16
F32 = jnp.float32
MESH = pl.DeviceIdType.MESH


def split(x):
    high = x.astype(BF)
    return high, (x - high.astype(F32)).astype(BF)


def mm(a, b):
    return jnp.dot(a, b, preferred_element_type=F32)


def pick(x, hot):
    high, low = split(x)
    both = mm(jnp.concatenate([high, low], axis=0), hot)
    return both[: x.shape[0]] + both[x.shape[0] :]


def apply_map(cat, x):
    high, low = split(x)
    return mm(cat, jnp.concatenate([high, high, low], axis=0))


def iota(shape, axis):
    return lax.broadcasted_iota(jnp.int32, shape, axis)


def kernel(
    n_line, n_sub, w_hbm, src_in, mmap_in, adm_in, att_in, past_in, code, span_in, owner_in,
    local_in, counts_in, out,
    src, mmap, adm, att, past, span, owner, local, counts, in_sem,
    w_flat, w_split, timeline, p_hot, pt_hot, q_hot, qt_hot, spread, map_cat, mapt_cat,
    source, admit, hist, inj_send, inj_recv, v_send, v_recv, sub_send, sub_recv,
    w_sem, inj_ss, inj_rs, v_ss, v_rs, sub_ss, sub_rs,
):
    me = lax.axis_index("line")
    grp = lax.axis_index("sub")
    cond, steps, buses = src.shape[1:]
    rows = TMIN * cond
    lines = adm.shape[2]
    depth = past.shape[0]
    subsets = w_hbm.shape[1]
    per = buses // subsets
    nodes = cond * per
    blocks = steps // TMIN
    cap = 2 * lines // n_line
    slots = n_line * cap
    parts = 128 // cap
    prow = rows // parts
    sent = -(-prow // 8) * 8

    barrier = pltpu.get_barrier_semaphore()
    for k in range(1, n_line):
        pl.semaphore_signal(
            barrier, inc=1, device_id={"line": lax.rem(me + k, n_line)}, device_id_type=MESH
        )
    for k in range(1, n_sub):
        pl.semaphore_signal(
            barrier, inc=1, device_id={"sub": lax.rem(grp + k, n_sub)}, device_id_type=MESH
        )
    w_copy = pltpu.make_async_copy(w_hbm.at[0], w_flat, w_sem)
    loads = [
        pltpu.make_async_copy(a, b, in_sem.at[i])
        for i, (a, b) in enumerate(
            [(owner_in, owner), (local_in, local), (span_in, span), (mmap_in, mmap), (past_in, past),
             (att_in, att), (adm_in, adm), (src_in, src), (counts_in, counts)]
        )
    ]
    for load in loads:
        load.start()
    w_copy.start()
    for load in loads[:6]:
        load.wait()

    def line_copy(send, recv, ss, rs, k, high=None):
        high = sent if high is None else high
        to = lax.rem(me + k, n_line)
        return pltpu.make_async_remote_copy(
            src_ref=send.at[to, 0:high], dst_ref=recv.at[me, 0:high], send_sem=ss.at[k], recv_sem=rs.at[k],
            device_id={"line": to}, device_id_type=MESH,
        )

    def line_wait(send, recv, ss, rs, high=None):
        high = sent if high is None else high
        for k in range(1, n_line):
            frm = lax.rem(me + n_line - k, n_line)
            pltpu.make_async_remote_copy(
                src_ref=send.at[frm, 0:high], dst_ref=recv.at[frm, 0:high], send_sem=ss.at[k], recv_sem=rs.at[k],
                device_id={"line": frm}, device_id_type=MESH,
            ).wait_recv()

    def line_sent(send, recv, ss, rs, high=None):
        for k in range(1, n_line):
            line_copy(send, recv, ss, rs, k, high).wait_send()

    def pack(x, send, recv):
        for d in range(n_line):
            send[d, 0:prow] = jnp.concatenate(
                [x[g * prow : (g + 1) * prow, d * cap : (d + 1) * cap] for g in range(parts)], axis=1
            )
        recv[me, 0:prow] = send[me, 0:prow]

    def unpack(recv):
        return jnp.concatenate(
            [
                jnp.concatenate(
                    [recv[d, 0:prow][:, g * cap : (g + 1) * cap] for d in range(n_line)], axis=1
                )
                for g in range(parts)
            ],
            axis=0,
        )

    def sub_copy(parity, k):
        return pltpu.make_async_remote_copy(
            src_ref=sub_send, dst_ref=sub_recv.at[parity, k - 1],
            send_sem=sub_ss.at[parity, k - 1], recv_sem=sub_rs.at[parity, k - 1],
            device_id={"sub": lax.rem(grp + k, n_sub)}, device_id_type=MESH,
        )

    hot_t = (iota((PAD, lines), 0) == owner[...]).astype(F32)
    upper = (iota((lines, lines), 0) < iota((lines, lines), 1)).astype(F32).astype(BF)
    earlier = mm(hot_t.astype(BF), upper)
    base = (iota((PAD, lines), 0) * cap).astype(F32)
    slot_row = jnp.sum(hot_t * (base + earlier), axis=0, keepdims=True).astype(jnp.int32)
    pt = (iota((slots, lines), 0) == slot_row).astype(F32)
    pt_hot[...] = pt.astype(BF)
    p_hot[...] = pt.T.astype(BF)

    stretch = (iota((rows, cond), 0) % cond == iota((rows, cond), 1)).astype(F32)
    same = (iota((rows, rows), 0) // cond == iota((rows, rows), 1) // cond).astype(F32)
    highest = lax.Precision.HIGHEST
    nt = (((1,), (1,)), ((), ()))

    def full(x):
        return lax.dot_general(x, stretch, nt, precision=highest, preferred_element_type=F32) * same

    fwd = full(jnp.dot(stretch, mmap[...], precision=highest, preferred_element_type=F32))

    def three(big):
        high, low = split(big)
        return jnp.concatenate(
            [high.astype(F32), low.astype(F32), high.astype(F32)], axis=1
        ).astype(BF)

    map_cat[...] = three(fwd)

    for i in range(depth):
        timeline[i * PAD : i * PAD + cond, :] = past[i, :, 0, :]
    damp = jnp.concatenate([att[:, 0, :], jnp.zeros((PAD - cond, lines), F32)], axis=0)
    span_row = span[...]

    def history(block):
        for t in range(TMIN):
            total = jnp.zeros((PAD, lines), F32)
            for d in range(depth - TMIN + 1):
                at = pl.multiple_of((block * TMIN + t + d) * PAD, PAD)
                total = jnp.where(span_row == depth - d, timeline[pl.ds(at, PAD), :], total)
            hist[t * cond : (t + 1) * cond, :] = (damp * total)[:cond]

    def start_inject(extra):
        inject = apply_map(map_cat[...], hist[...])
        if extra is not None:
            both = jnp.concatenate([inject, jnp.broadcast_to(extra, (16, lines))], axis=0)
            both = pick(both, p_hot[...])
            inject = both[:rows]
            for d in range(n_line):
                piece = both[rows : rows + 8, d * cap : (d + 1) * cap]
                inj_send[d, sent : sent + 8] = jnp.concatenate([piece] * parts, axis=1)
            inj_recv[me, sent : sent + 8] = inj_send[me, sent : sent + 8]
        else:
            inject = pick(inject, p_hot[...])
        pack(inject, inj_send, inj_recv)

    history(0)
    if sent > prow:
        inj_send[...] = jnp.zeros_like(inj_send)
        v_send[...] = jnp.zeros_like(v_send)
    start_inject(local[...].astype(F32))
    pl.semaphore_wait(barrier, n_line - 1 + n_sub - 1)
    for k in range(1, n_line):
        line_copy(inj_send, inj_recv, inj_ss, inj_rs, k, sent + 8).start()

    for load in loads[6:]:
        load.wait()
    mapt_cat[...] = three(
        full(lax.dot_general(stretch, mmap[...], nt, precision=highest, preferred_element_type=F32))
    )
    r, s = iota((2 * WIDE, cond * 128), 0), iota((2 * WIDE, cond * 128), 1)
    r_in, s_in = r & (WIDE - 1), s & (WIDE - 1)
    spread[...] = (
        (r // WIDE == (s & 127) // WIDE) & (r_in // cond == s_in // cond)
        & (r_in % cond == s // 128)
    ).astype(F32).astype(BF)
    expand = (iota((subsets, buses), 0) == iota((subsets, buses), 1) // per).astype(F32).astype(BF)
    count_row = mm(
        jnp.broadcast_to(counts[...].astype(F32), (8, subsets)).astype(BF), expand
    )[0:1]
    slot_in = (iota((1, buses), 1) & (per - 1)).astype(F32)
    live = (slot_in < count_row).astype(F32)
    for t in range(steps):
        source[t * cond : (t + 1) * cond, :] = src[0, :, t, :]
    admit[...] = jnp.concatenate([2.0 * adm[:, 0, :]] * TMIN, axis=0)
    w_copy.wait()

    def relayout(n, carry):
        at = pl.multiple_of(n * (16 * nodes), 128)
        wide = w_flat[:, pl.ds(at, 16 * nodes)]
        cube = jnp.stack([wide[:, i * nodes : (i + 1) * nodes] for i in range(16)], axis=0)
        turned = jnp.transpose(cube, (1, 0, 2))
        high, low = split(turned)
        here = pl.multiple_of(n * 16, 16)
        w_split[:, pl.ds(here, 16), :] = high
        w_split[:, pl.ds(pl.multiple_of(nodes + here, 16), 16), :] = low
        return carry

    lax.fori_loop(0, nodes // 16, relayout, 0)
    partner = lax.bitwise_xor(grp, code[0])

    line_wait(inj_send, inj_recv, inj_ss, inj_rs, sent + 8)
    line_sent(inj_send, inj_recv, inj_ss, inj_rs, sent + 8)
    id_row = jnp.concatenate(
        [inj_recv[d, sent : sent + 8][0:1, 0:cap] for d in range(n_line)], axis=1
    )
    qt = (iota((buses, slots), 0).astype(F32) == id_row).astype(F32)
    qt_hot[...] = qt.astype(BF)
    q_hot[...] = qt.T.astype(BF)
    diag = (iota((per, 128), 1) & (WIDE - 1)) % cond

    def one_block(block, carry):
        at = pl.multiple_of(block * rows, 8)
        summed = pick(unpack(inj_recv), q_hot[...])
        right = (summed + source[pl.ds(at, rows), :]) * live
        high, low = split(right)
        gap = jnp.zeros((WIDE - rows, buses), F32)
        both = jnp.concatenate([high.astype(F32), gap, low.astype(F32), gap], axis=0)
        wide = mm(both.T.astype(BF), spread[...]).astype(BF)
        pieces = []
        for g in range(subsets):
            x = jnp.concatenate(
                [wide[g * per : (g + 1) * per, c * 128 : (c + 1) * 128] for c in range(cond)], axis=0
            )
            y = mm(w_split[g], x)
            y = y[:nodes] + y[nodes:]
            total = jnp.zeros((per, 128), F32)
            for c in range(cond):
                total = jnp.where(diag == c, y[c * per : (c + 1) * per], total)
            pieces.append(total)
        turned = jnp.concatenate(pieces, axis=0).T
        volts = (turned[:rows] + turned[WIDE : WIDE + rows]) * live
        for t in range(TMIN):
            out[0, block * TMIN + t] = volts[t * cond : (t + 1) * cond]

        @pl.when(block < blocks - 1)
        def _():
            pack(pick(volts, qt_hot[...]), v_send, v_recv)
            for k in range(1, n_line):
                line_copy(v_send, v_recv, v_ss, v_rs, k).start()
            line_wait(v_send, v_recv, v_ss, v_rs)
            modal = apply_map(mapt_cat[...], pick(unpack(v_recv), pt_hot[...]))
            sub_send[...] = admit[...] * modal - hist[...]
            parity = lax.rem(block, 2)
            for k in range(1, n_sub):
                sub_copy(parity, k).start()
            arrived = jnp.zeros((rows, lines), F32)
            for k in range(1, n_sub):
                sub_copy(parity, k).wait_recv()
                frm = lax.rem(grp + n_sub - k, n_sub)
                arrived = jnp.where(partner == frm, sub_recv[parity, k - 1], arrived)
            gap = jnp.zeros((PAD - cond, lines), F32)
            for t in range(TMIN):
                here = pl.multiple_of((depth + block * TMIN + t) * PAD, PAD)
                timeline[pl.ds(here, PAD), :] = jnp.concatenate(
                    [arrived[t * cond : (t + 1) * cond], gap], axis=0
                )
            history(block + 1)
            start_inject(None)
            for k in range(1, n_line):
                line_copy(inj_send, inj_recv, inj_ss, inj_rs, k).start()
            line_sent(v_send, v_recv, v_ss, v_rs)
            for k in range(1, n_sub):
                sub_copy(parity, k).wait_send()
            line_wait(inj_send, inj_recv, inj_ss, inj_rs)
            line_sent(inj_send, inj_recv, inj_ss, inj_rs)

        return carry

    lax.fori_loop(0, blocks, one_block, 0)


def per_device(
    nodal_inverse, bus_source, modal_map, admittance, attenuation, past_waves, tie_code,
    travel_span, bus_owner, bus_local, bus_count,
):
    n_line, n_sub = lax.axis_size("line"), lax.axis_size("sub")
    _, steps, cond, buses = bus_source.shape
    lines = admittance.shape[2]
    depth = past_waves.shape[1]
    subsets = nodal_inverse.shape[1]
    nodes = cond * (buses // subsets)
    cap = 2 * lines // n_line
    slots = n_line * cap
    rows = TMIN * cond
    sent = -(-(rows * cap // 128) // 8) * 8
    vmem = pl.BlockSpec(memory_space=pltpu.VMEM)
    hbm = pl.BlockSpec(memory_space=pl.ANY)
    smem = pl.BlockSpec(memory_space=pltpu.SMEM)
    dma = pltpu.SemaphoreType.DMA
    return pl.pallas_call(
        functools.partial(kernel, n_line, n_sub),
        out_shape=jax.ShapeDtypeStruct(bus_source.shape, F32),
        in_specs=[hbm] * 6 + [smem] + [hbm] * 4,
        out_specs=vmem,
        scratch_shapes=[
            pltpu.VMEM((1, cond, steps, buses), F32),
            pltpu.VMEM((cond, cond), F32),
            pltpu.VMEM((cond, 1, lines), F32),
            pltpu.VMEM((cond, 1, lines), F32),
            pltpu.VMEM((depth, cond, 1, lines), F32),
            pltpu.VMEM((1, lines), jnp.int32),
            pltpu.VMEM((1, lines), jnp.int32),
            pltpu.VMEM((1, lines), jnp.int32),
            pltpu.VMEM((1, subsets), jnp.int32),
            dma((9,)),
            pltpu.VMEM((subsets, nodes * nodes), F32),
            pltpu.VMEM((subsets, 2 * nodes, nodes), BF),
            pltpu.VMEM(((depth + steps) * PAD, lines), F32),
            pltpu.VMEM((lines, slots), BF),
            pltpu.VMEM((slots, lines), BF),
            pltpu.VMEM((slots, buses), BF),
            pltpu.VMEM((buses, slots), BF),
            pltpu.VMEM((2 * WIDE, cond * 128), BF),
            pltpu.VMEM((rows, 3 * rows), BF),
            pltpu.VMEM((rows, 3 * rows), BF),
            pltpu.VMEM((steps * cond, buses), F32),
            pltpu.VMEM((rows, lines), F32),
            pltpu.VMEM((rows, lines), F32),
            pltpu.VMEM((n_line, sent + 8, 128), F32),
            pltpu.VMEM((n_line, sent + 8, 128), F32),
            pltpu.VMEM((n_line, sent, 128), F32),
            pltpu.VMEM((n_line, sent, 128), F32),
            pltpu.VMEM((rows, lines), F32),
            pltpu.VMEM((2, n_sub - 1, rows, lines), F32),
            dma,
            dma((n_line,)), dma((n_line,)), dma((n_line,)), dma((n_line,)),
            dma((2, n_sub - 1)), dma((2, n_sub - 1)),
        ],
        compiler_params=pltpu.CompilerParams(
            collective_id=0, has_side_effects=True, vmem_limit_bytes=56 * 1024 * 1024
        ),
    )(
        nodal_inverse, jnp.transpose(bus_source, (0, 2, 1, 3)), modal_map,
        jnp.transpose(admittance, (1, 0, 2)), jnp.transpose(attenuation, (1, 0, 2)),
        jnp.transpose(past_waves, (1, 2, 0, 3)), tie_code, travel_span, bus_owner[:, :, 0], bus_local, bus_count,
    )


def solution(mesh):
    in_specs = (
        P("sub", "line", None),
        P("sub", None, None, "line"),
        P(),
        P("sub", None, "line"),
        P("sub", None, "line"),
        P("sub", None, None, "line"),
        P("line"),
        P("sub", "line"),
        P("sub", "line", None),
        P("sub", "line"),
        P("sub", "line"),
    )
    out_specs = P("sub", None, None, "line")
    return jax.shard_map(
        per_device, mesh=mesh, in_specs=in_specs, out_specs=out_specs, check_vma=False
    )
```
